32 devices in a mesh: groups: 2 (over x), rep: 2 (over core), tp: 8 (over z, y).
Axes of the slice: x: 2, y: 2, z: 4, core: 2. Of those that a mesh axis runs over, the one named last changes fastest.
Arguments:
- hidden: bfloat16 [1024, 2, 28672], P(('groups', 'rep'), None, 'tp'), parts along dimension 0, may hold values from -6 to 6
- down_weight: bfloat16 [28672, 8192], P('tp'), may hold values from -0.046875 to 0.046875
- residual: bfloat16 [1024, 2, 8192], P(('groups', 'rep'), None, 'tp'), parts along dimension 0, may hold values from -6 to 6
- pool_shrink: bfloat16 [16, 8, 64, 3584], P(('rep', 'tp')), may hold values from -0.03125 to 0.03125
- pool_expand: bfloat16 [16, 8, 64, 1024], P(('rep', 'tp')), may hold values from -0.75 to 0.75
- tenant_home: int32 [16], replicated, may hold values from 0 to 15, each once
- request_owner_tenant: int32 [1024, 1], P(('groups', 'rep')), parts along dimension 0, may hold values from 0 to 15; in each aligned block of 256 rows (0 to 255, 256 to 511, ...) at most 64 rows name the same one
Outputs:
- mixed: bfloat16 [1024, 2, 8192], P(('groups', 'rep'), None, 'tp'), parts along dimension 0
The draws below stay inside these ranges and needn't reach their ends.
There are 2 independent parts, one for each index of `groups`. The reference program is written for one: setup_inputs(seed, part) draws one part's arguments, and reference() takes and returns one part's arrays. A program takes and returns all parts, laid end to end along the dimension named above; an argument that names none is the same for every part. Nothing has to cross between parts.
Inputs may be any that keep to these rules, and one draw needn't show every extreme that they name: `request_owner_tenant`: among the 256 requests of one replica no tenant appears more than 64 times, and in some replica one tenant appears exactly 64 times; every tenant appears in some request. `tenant_home`: each tenant has its own home.
All inputs are finite; a program needn't handle non-finite values.
Results may differ from the reference program's by a relative error of at most 0.0033.
Values may be sent and summed in bfloat16 or wider, within the bound.
A program may use at most 448 MiB of HBM per device.

```python
import math
import jax
import jax.numpy as jnp
import numpy as np
from jax import lax

D = 8192
FF = 28672
RANK = 64
STEPS = 2
REQ_DEV = 256
TENANTS = 16
REQUESTS = 512
MOST = 64
N_TP = 8


def with_spikes(values, key, source, target, shards_of, factor):
    owner, partner = [(jnp.arange(values.shape[position]) // (values.shape[position] // shards_of)).reshape([-1 if axis == position else 1 for axis in range(values.ndim)]) for position in (source, target)]
    chosen = jax.random.permutation(key, shards_of)[partner]
    strong = (owner == chosen) | (owner == (partner + shards_of // 2) % shards_of)
    return jnp.where(strong, factor * values, values)


def levels(key, extent, split, low, top_value):
    factor_of = 1.0
    for position, blocks in split:
        heights = jax.random.uniform(jax.random.fold_in(jax.random.fold_in(key, 6), position), (blocks,), jnp.float32, low / len(split), top_value / len(split))
        factor_of = factor_of * jnp.repeat(jnp.exp(heights), extent[position] // blocks).reshape((-1,) + (1,) * (len(extent) - 1 - position))
    return factor_of


def routed_block(stream_key, own, number, rows, number_of, top, most, lean):
    sequence = jax.random.permutation(stream_key, number_of)
    heavy_load, common = shares(number_of, rows * top, most, lean, True), shares(number_of, rows * top, most, lean, False)
    places = jnp.arange(number_of)

    def named(tallies, turn):
        used = int((tallies > 0).sum())
        fixed = max(1, used // 4)
        moved = fixed + (places - fixed + turn * (used - fixed)) % max(1, number_of - fixed)
        return jnp.zeros((number_of,), jnp.int32).at[sequence[jnp.where(places < fixed, places, moved)]].set(jnp.asarray(tallies, jnp.int32))

    tallies = jnp.where(number % 4 == 0, named(heavy_load, number // 4), named(common, number - number // 4 - 1))
    mixed = jax.random.permutation(jax.random.fold_in(own, 3), number_of)
    giver, taker = mixed[0:number_of // 2 * 2:2], mixed[1:number_of // 2 * 2:2]
    slack = jnp.minimum(tallies[giver] - 1, most - tallies[taker]) // 2
    slack = jnp.where((giver == sequence[0]) | (taker == sequence[0]) | (tallies[taker] == 0), 0, jnp.maximum(slack, 0))
    moved = jax.random.randint(jax.random.fold_in(own, 4), (number_of // 2,), 0, 1 << 20) % (slack + 1)
    tallies = tallies.at[giver].add(-moved).at[taker].add(moved)
    labels = jnp.searchsorted(jnp.cumsum(tallies), jnp.arange(rows * top), side="right").astype(jnp.int32)
    grid = labels.reshape(top, rows).T
    grid = grid[jax.random.permutation(jax.random.fold_in(own, 1), rows)]
    turn = jax.random.randint(jax.random.fold_in(own, 2), (rows, 1), 0, top)
    return jnp.take_along_axis(grid, (jnp.arange(top)[None, :] + turn) % top, axis=1)


def shares(number_of, total, most, slope, full):
    loads = [(1 << 20) // math.isqrt(rank ** slope) + 1 for rank in range(1, number_of + 1)]
    largest = most if full else min(most, max(-(-total // number_of), total * loads[0] // sum(loads)))
    least = 1 if total - largest >= number_of - 1 else 0
    given, spare = [largest] + [least] * (number_of - 1), total - largest - least * (number_of - 1)
    while spare > 0:
        candidates = [i for i in range(1, number_of) if given[i] < largest] or [i for i in range(1, number_of) if given[i] < most]
        whole, remaining = sum([loads[i] for i in candidates]), spare
        for i in candidates:
            more = min(most - given[i], max(1, remaining * loads[i] // whole), spare)
            given[i] = given[i] + more
            spare = spare - more
    return np.array(given)


def noise(key, extent, spread, bound, split=(), kind=jnp.bfloat16):
    entries = spread * jax.random.normal(key, extent, jnp.float32)
    if split:
        entries = entries * levels(key, extent, split, -0.22, 0.18)
    return jnp.clip(entries, -bound, bound).astype(kind)


def bell_draw_with(stream_key, shape, spread, bound, cuts, heavy, kind=jnp.bfloat16):
    drawn = spread * jax.random.normal(stream_key, shape, jnp.float32)
    if cuts:
        drawn = drawn * levels(stream_key, shape, cuts, -0.22, 0.18)
    return jnp.clip(with_spikes(drawn, jax.random.fold_in(stream_key, 3), *heavy), -bound, bound).astype(kind)


def setup_inputs(seed: int = 0, part: int = 0) -> dict:
    key_list = jax.random.split(jax.random.key(seed), 8)
    part_splits = jax.random.split(jax.random.fold_in(key_list[7], part), 8)
    hidden = noise(part_splits[0], (REQUESTS, STEPS, FF), 1.0, 6.0, ((0, 2), (2, 8)))
    down_weight = bell_draw_with(key_list[1], (FF, D), FF ** -0.5, 0.046875, ((0, 8),), (0, 1, 8, 2.0))
    residual = noise(part_splits[2], (REQUESTS, STEPS, D), 1.0, 6.0, ((0, 2), (2, 8)))
    pool_shrink = noise(key_list[3], (TENANTS, N_TP, RANK, FF // N_TP), FF ** -0.5, 0.03125, ((0, 16),))
    pool_expand = noise(key_list[4], (TENANTS, N_TP, RANK, D // N_TP), RANK ** -0.5, 0.75, ((0, 16),))
    tenant_home = jax.random.permutation(key_list[5], TENANTS).astype(jnp.int32)
    request_owner_tenant_keys = jax.random.split(jax.random.fold_in(part_splits[6], 1), REQUESTS // REQ_DEV)
    request_owner_tenant_turns = jax.random.permutation(jax.random.fold_in(part_splits[6], 3), REQUESTS // REQ_DEV)
    request_owner_tenant = jax.vmap(lambda own, number: routed_block(jax.random.fold_in(part_splits[6], 2), own, number, REQ_DEV, TENANTS, 1, MOST, 2))(request_owner_tenant_keys, request_owner_tenant_turns).reshape((REQUESTS, 1))
    return {"hidden": hidden, "down_weight": down_weight, "residual": residual, "pool_shrink": pool_shrink, "pool_expand": pool_expand, "tenant_home": tenant_home, "request_owner_tenant": request_owner_tenant}


def reference(hidden, down_weight, residual, pool_shrink, pool_expand, tenant_home, request_owner_tenant):
    unit_width = FF // N_TP
    base_output = jnp.dot(hidden.reshape(REQUESTS * STEPS, FF), down_weight, preferred_element_type=jnp.float32)
    base_output = base_output.reshape(REQUESTS, STEPS, D)
    blocks = jnp.arange(N_TP, dtype=jnp.int32)

    def single_request(item):
        rows, tenant = item
        home = tenant_home[tenant]
        holder = (home // N_TP) * N_TP + (home % N_TP + blocks) % N_TP
        shrink_map = pool_shrink[holder, blocks]
        expand_map = pool_expand[holder, blocks]
        grouped = rows.reshape(STEPS, N_TP, unit_width).astype(jnp.float32)
        codes = jnp.einsum("sjf,jkf->sk", grouped, shrink_map.astype(jnp.float32))
        codes = lax.optimization_barrier(codes.astype(jnp.bfloat16))
        adapted = jnp.einsum("sk,jkc->sjc", codes.astype(jnp.float32), expand_map.astype(jnp.float32))
        return adapted.reshape(STEPS, D)

    adapter_output = lax.map(single_request, (hidden, request_owner_tenant[:, 0]))
    return (residual.astype(jnp.float32) + base_output + adapter_output).astype(jnp.bfloat16)
```

```python
import functools
import math

import jax
import jax.numpy as jnp
from jax import lax
from jax.experimental import pallas as pl
from jax.experimental.pallas import tpu as pltpu
from jax.sharding import PartitionSpec as P

MESH = pl.DeviceIdType.MESH
F32 = jnp.float32
BF16 = jnp.bfloat16


def fused(
    tp, lo, hi, tile, sub,
    hidden, weight, shrink, expand, source, out,
    w_buf, y_send, y_recv, keep, z_send, z_recv, a_buf, e_buf, part, part_in, code, code_own,
    w_sem, y_ssem, y_rsem, z_ssem, z_rsem, a_sems, e_sems, c_sems,
):
    g, r, p = lax.axis_index("groups"), lax.axis_index("rep"), lax.axis_index("tp")
    z, y = p // lo, p % lo
    rows = hidden.shape[0]
    width = out.shape[1]
    per = width // tile
    units = hi * per
    rank = shrink.shape[2]
    half = rank // 2
    share = rows // tp
    across, sibling = {"groups": 1 - g}, {"rep": 1 - r}

    def remote(src, dst, ssem, rsem, device):
        return pltpu.make_async_remote_copy(
            src_ref=src, dst_ref=dst, send_sem=ssem, recv_sem=rsem,
            device_id=device, device_id_type=MESH,
        )

    def loop(n, body):
        lax.fori_loop(0, n, lambda i, c: (body(i), c)[1], 0)

    def peer(j):
        return {"tp": (p + j) % tp}

    barrier = pltpu.get_barrier_semaphore()
    loop(tp - 1, lambda j: pl.semaphore_signal(
        barrier, inc=1, device_id=peer(j + 1), device_id_type=MESH))
    pl.semaphore_signal(barrier, inc=1, device_id=across, device_id_type=MESH)
    pl.semaphore_signal(barrier, inc=1, device_id=sibling, device_id_type=MESH)

    def unit(i):
        q, c = i // per, i % per
        zz = jnp.where(q % 2 == 0, hi - 1 - q // 2, q // 2)
        return zz, c

    sends = units * (lo - 1)
    total = units * lo

    def tile_of(n):
        sending = n < sends
        i = jnp.where(sending, n // max(lo - 1, 1), n - sends)
        j = jnp.where(sending, 1 + n % max(lo - 1, 1), 0)
        zz, c = unit(i)
        return zz, c, j

    def w_copy(n):
        zz, c, j = tile_of(n)
        column = (zz * lo + (y + j) % lo) * width + c * tile
        return pltpu.make_async_copy(
            weight.at[:, pl.ds(pl.multiple_of(column, tile), tile)],
            w_buf.at[n % 2], w_sem.at[n % 2],
        )

    w_copy(0).start()
    pl.semaphore_wait(barrier, tp + 1)

    mine = pl.ds(pl.multiple_of(g * half, half), half)
    other = pl.ds(pl.multiple_of((1 - g) * half, half), half)

    def page_copies(j):
        k = (p + j) % tp
        return [
            remote(pool.at[0, k, mine], buf.at[r, p, mine], s.at[0, k], s.at[1, p], {"tp": k})
            for pool, buf, s in ((shrink, a_buf, a_sems), (expand, e_buf, e_sems))
        ]

    def own_copies():
        return [
            pltpu.make_async_copy(pool.at[0, p, mine], buf.at[r, p, mine], s.at[1, p])
            for pool, buf, s in ((shrink, a_buf, a_sems), (expand, e_buf, e_sems))
        ]

    def across_copies(src, rows_of):
        return [
            remote(buf.at[r, src, rows_of], buf.at[r, src, rows_of],
                   s.at[2, src], s.at[3, src], across)
            for buf, s in ((a_buf, a_sems), (e_buf, e_sems))
        ]

    def sibling_copies(rep, src):
        return [
            remote(buf.at[rep, src], buf.at[rep, src], s.at[4, src], s.at[5, src], sibling)
            for buf, s in ((a_buf, a_sems), (e_buf, e_sems))
        ]

    def start_pages(j):
        for copy in page_copies(j + 1):
            copy.start()

    for copy in own_copies():
        copy.start()
    loop(tp - 1, start_pages)

    def product(n, store):
        @pl.when(n + 1 < total)
        def _():
            w_copy(n + 1).start()

        w_copy(n).wait()

        def piece(t):
            columns = pl.ds(pl.multiple_of(t * sub, sub), sub)
            store(columns, jnp.dot(
                hidden[...], w_buf[n % 2, :, columns], preferred_element_type=F32))

        loop(tile // sub, piece)

    def y_copy(u, j):
        device = {"tp": z * lo + (y + j) % lo}
        return remote(y_send.at[u, j - 1], y_recv.at[u, j - 1],
                      y_ssem.at[u, j - 1], y_rsem.at[u, j - 1], device)

    def send_tile(n):
        zz, c, j = tile_of(n)
        u = zz * per + c

        def store(columns, value):
            y_send[u, j - 1, :, columns] = value.astype(BF16)

        product(n, store)
        y_copy(u, j).start()

    loop(sends, send_tile)

    def forward(j):
        src = (p + tp - j) % tp

        @pl.when(j == 0)
        def _():
            for copy in own_copies():
                copy.wait()

        @pl.when(j > 0)
        def _():
            for pool, buf, s in ((shrink, a_buf, a_sems), (expand, e_buf, e_sems)):
                remote(pool.at[0, src, mine], buf.at[r, src, mine],
                       s.at[0, src], s.at[1, src], {"tp": src}).wait_recv()

        for copy in across_copies(src, mine):
            copy.start()

    def keep_tile(i):
        zz, c = unit(i)
        u = zz * per + c

        def store(columns, value):
            keep[u, :, columns] = value

        product(sends + i, store)
        loop(tp // units, lambda t: forward(i * (tp // units) + t))

    loop(units, keep_tile)

    def base(u):
        value = keep[u]
        for j in range(1, lo):
            value = value + y_recv[u, j - 1].astype(F32)
        return value

    def wait_y(u):
        for j in range(1, lo):
            y_copy(u, j).wait_recv()

    def z_copy(u, zz, c):
        nz = jnp.where(zz > z, z + 1, z - 1)
        slot = jnp.where((nz == zz) & (zz < z), units + c, u)
        return remote(z_send.at[u], z_recv.at[slot], z_ssem.at[u], z_rsem.at[slot],
                      {"tp": nz * lo + y})

    def z_arrived(slot):
        remote(z_send.at[0], z_recv.at[slot], z_ssem.at[0], z_rsem.at[slot],
               across).wait_recv()

    def pass_on(i):
        zz, c = unit(i)
        u = zz * per + c
        first = jnp.where(zz > z, z == 0, z == hi - 1)

        @pl.when(zz != z)
        def _():
            wait_y(u)

            @pl.when(first)
            def _():
                z_send[u] = base(u).astype(BF16)

            @pl.when(jnp.logical_not(first))
            def _():
                z_arrived(u)
                z_send[u] = (base(u) + z_recv[u].astype(F32)).astype(BF16)

            z_copy(u, zz, c).start()

    def share_page(j):
        src = (p + tp - j) % tp
        for copy in across_copies(src, other):
            copy.wait_recv()
        for copy in sibling_copies(r, src):
            copy.start()

    early = units // 2
    loop(early, pass_on)
    loop(tp, share_page)

    def wait_page(j):
        src = (p + tp - j) % tp
        for copy in sibling_copies(1 - r, src):
            copy.wait_recv()

    loop(tp, wait_page)
    quads = tp // 4
    lane = lax.broadcasted_iota(jnp.int32, (rows, 4 * rank), 1) // rank

    def chosen(i):
        return source[...] == lane + i * 4

    def shrink_quad(i):
        pages = a_buf[i // quads, pl.ds((i % quads) * 4, 4)].reshape(4 * rank, a_buf.shape[3])
        value = lax.dot_general(
            hidden[...], pages, (((1,), (1,)), ((), ())), preferred_element_type=F32)
        part[...] += jnp.where(chosen(i), value, 0.0)

    part[...] = jnp.zeros_like(part)
    loop(2 * quads, shrink_quad)
    folded = part[:, :2 * rank] + part[:, 2 * rank:]
    folded = folded + jnp.concatenate([folded[:, rank:], folded[:, :rank]], axis=1)
    part[:, :2 * rank] = folded

    def rows_of(k):
        return pl.ds(pl.multiple_of(k * share, share), share)

    def part_copy(j):
        k = (p + j) % tp
        return remote(part.at[rows_of(k), pl.ds(0, 2 * rank)], part_in.at[p],
                      c_sems.at[0, k], c_sems.at[1, p], {"tp": k})

    def part_arrived(src):
        return remote(part.at[rows_of(src), pl.ds(0, 2 * rank)], part_in.at[src],
                      c_sems.at[0, src], c_sems.at[1, src], {"tp": src})

    def code_copy(k, at):
        return remote(code_own, code.at[rows_of(at)],
                      c_sems.at[2, k], c_sems.at[3, at], {"tp": k})

    loop(tp - 1, lambda j: part_copy(j + 1).start())
    loop(units - early, lambda i: pass_on(early + i))

    code_own[...] = part[rows_of(p), :2 * rank]

    def add_part(j):
        src = (p + j + 1) % tp
        part_arrived(src).wait_recv()
        code_own[...] += part_in[src]

    loop(tp - 1, add_part)
    code_own[...] = code_own[...].astype(BF16).astype(F32)
    code[rows_of(p), :] = code_own[...]
    loop(tp - 1, lambda j: code_copy((p + j + 1) % tp, p).start())
    loop(tp - 1, lambda j: code_copy((p + j + 1) % tp, (p + j + 1) % tp).wait_recv())

    out[...] = jnp.zeros_like(out)

    def expand_quad(i):
        both = code[...]
        codes = jnp.where(chosen(i), jnp.concatenate([both, both], axis=1), 0.0).astype(BF16)
        pages = e_buf[i // quads, pl.ds((i % quads) * 4, 4)].reshape(4 * rank, width)
        out[...] += jnp.dot(codes, pages, preferred_element_type=F32)

    loop(2 * quads, expand_quad)

    def finish(c):
        u = z * per + c
        columns = pl.ds(pl.multiple_of(c * tile, tile), tile)
        wait_y(u)
        out[:, columns] += base(u)

        @pl.when(z > 0)
        def _():
            z_arrived(u)
            out[:, columns] += z_recv[u].astype(F32)

        @pl.when(z < hi - 1)
        def _():
            z_arrived(units + c)
            out[:, columns] += z_recv[units + c].astype(F32)

    loop(per, finish)

    def sent(i):
        zz, c = unit(i)
        u = zz * per + c
        for j in range(1, lo):
            y_copy(u, j).wait_send()

        @pl.when(zz != z)
        def _():
            z_copy(u, zz, c).wait_send()

    loop(units, sent)

    def sent_pages(j):
        for copy in across_copies(j, mine) + sibling_copies(r, j):
            copy.wait_send()

        @pl.when(j > 0)
        def _():
            for copy in page_copies(j):
                copy.wait_send()
            part_copy(j).wait_send()
            code_copy((p + j) % tp, p).wait_send()

    loop(tp, sent_pages)


def per_device(
    hidden, down_weight, residual, pool_shrink, pool_expand, tenant_home, request_owner_tenant
):
    tp = lax.axis_size("tp")
    reps = lax.axis_size("rep")
    place = lax.axis_index("tp")
    requests, steps, units = hidden.shape
    width = residual.shape[2]
    rank = pool_shrink.shape[2]
    rows = requests * steps
    home_device = tenant_home // tp * tp + (tenant_home % tp + place) % tp
    tenants = tenant_home.shape[0]
    source = jnp.sum(
        jnp.where(request_owner_tenant == jnp.arange(tenants)[None, :], home_device[None, :], 0),
        axis=1, dtype=jnp.int32,
    )
    source = jnp.broadcast_to(source[:, None], (requests, steps)).reshape(rows, 1)
    lo = 1 << (int(math.log2(tp)) // 2)
    hi = tp // lo
    tile = min(512, width)
    sub = min(256, tile)
    per = width // tile
    n = hi * per
    dma = pltpu.SemaphoreType.DMA
    vmem = pl.BlockSpec(memory_space=pltpu.VMEM)
    hbm = pl.BlockSpec(memory_space=pl.ANY)
    added = pl.pallas_call(
        functools.partial(fused, tp, lo, hi, tile, sub),
        out_shape=jax.ShapeDtypeStruct((rows, width), F32),
        in_specs=[vmem, hbm, hbm, hbm, vmem],
        out_specs=vmem,
        scratch_shapes=[
            pltpu.VMEM((2, units, tile), BF16),
            pltpu.VMEM((n, lo - 1, rows, tile), BF16),
            pltpu.VMEM((n, lo - 1, rows, tile), BF16),
            pltpu.VMEM((n, rows, tile), F32),
            pltpu.VMEM((n, rows, tile), BF16),
            pltpu.VMEM((n + per, rows, tile), BF16),
            pltpu.VMEM((reps, tp, rank, units), BF16),
            pltpu.VMEM((reps, tp, rank, width), BF16),
            pltpu.VMEM((rows, 4 * rank), F32),
            pltpu.VMEM((tp, rows // tp, 2 * rank), F32),
            pltpu.VMEM((rows, 2 * rank), F32),
            pltpu.VMEM((rows // tp, 2 * rank), F32),
            dma((2,)),
            dma((n, lo - 1)),
            dma((n, lo - 1)),
            dma((n,)),
            dma((n + per,)),
            dma((6, tp)),
            dma((6, tp)),
            dma((4, tp)),
        ],
        compiler_params=pltpu.CompilerParams(
            collective_id=0, has_side_effects=True, vmem_limit_bytes=62 * 1024 * 1024
        ),
    )(hidden.reshape(rows, units), down_weight, pool_shrink, pool_expand, source)
    added = added.reshape(requests, steps, width)
    return (residual.astype(F32) + added).astype(BF16)


def solution(mesh):
    in_specs = (
        P(("groups", "rep"), None, "tp"),
        P("tp", None),
        P(("groups", "rep"), None, "tp"),
        P(("rep", "tp"), None, None, None),
        P(("rep", "tp"), None, None, None),
        P(),
        P(("groups", "rep"), None),
    )
    out_specs = P(("groups", "rep"), None, "tp")
    return jax.shard_map(
        per_device, mesh=mesh, in_specs=in_specs, out_specs=out_specs, check_vma=False
    )
```

```python
import functools
import math

import jax
import jax.numpy as jnp
from jax import lax
from jax.experimental import pallas as pl
from jax.experimental.pallas import tpu as pltpu
from jax.sharding import PartitionSpec as P

MESH = pl.DeviceIdType.MESH
F32 = jnp.float32
BF16 = jnp.bfloat16


def fused(
    tp, lo, hi, tile, sub, zf,
    hidden, weight, shrink, expand, source, out,
    w_buf, y_send, y_recv, keep, z_send, z_recv, f_own, f_send, f_recv, fy_send, fy_recv, a_buf, e_buf, part, part_in, code, code_own,
    w_sem, y_ssem, y_rsem, z_ssem, z_rsem, f_ssem, f_rsem, fy_sems, a_sems, e_sems, c_sems,
):
    g, r, p = lax.axis_index("groups"), lax.axis_index("rep"), lax.axis_index("tp")
    z, y = p // lo, p % lo
    rows = hidden.shape[0]
    width = out.shape[1]
    per = width // tile - zf
    units = hi * per
    firsts = tp * zf
    rank = shrink.shape[2]
    half = rank // 2
    share = rows // tp
    across, sibling = {"groups": 1 - g}, {"rep": 1 - r}

    def remote(src, dst, ssem, rsem, device):
        return pltpu.make_async_remote_copy(
            src_ref=src, dst_ref=dst, send_sem=ssem, recv_sem=rsem,
            device_id=device, device_id_type=MESH,
        )

    def loop(n, body):
        lax.fori_loop(0, n, lambda i, c: (body(i), c)[1], 0)

    def peer(j):
        return {"tp": (p + j) % tp}

    barrier = pltpu.get_barrier_semaphore()
    loop(tp - 1, lambda j: pl.semaphore_signal(
        barrier, inc=1, device_id=peer(j + 1), device_id_type=MESH))
    pl.semaphore_signal(barrier, inc=1, device_id=across, device_id_type=MESH)
    pl.semaphore_signal(barrier, inc=1, device_id=sibling, device_id_type=MESH)

    def far(q):
        return jnp.where(q % 2 == 0, hi - 1 - q // 2, q // 2)

    def unit(i):
        return far(i // per), i % per

    def first_unit(m):
        rest = m % (lo * zf)
        return far(m // (lo * zf)), rest // zf, rest % zf

    sends = units * (lo - 1)
    total = units * lo + firsts

    def column_of(n):
        sending = n < sends
        i = jnp.where(sending, n // (lo - 1), jnp.maximum(n - sends - firsts, 0))
        zz, c = unit(i)
        yy = jnp.where(sending, (y + 1 + n % (lo - 1)) % lo, y)
        if zf:
            m = jnp.clip(n - sends, 0, firsts - 1)
            fz, fy, fc = first_unit(m)
            inside = jnp.logical_and(n >= sends, n < sends + firsts)
            zz = jnp.where(inside, fz, zz)
            yy = jnp.where(inside, fy, yy)
            c = jnp.where(inside, per + fc, c)
        return (zz * lo + yy) * width + c * tile

    def w_copy(n):
        return pltpu.make_async_copy(
            weight.at[:, pl.ds(pl.multiple_of(column_of(n), tile), tile)],
            w_buf.at[n % 2], w_sem.at[n % 2],
        )

    w_copy(0).start()
    pl.semaphore_wait(barrier, tp + 1)

    mine = pl.ds(pl.multiple_of(g * half, half), half)
    other = pl.ds(pl.multiple_of((1 - g) * half, half), half)

    def page_copies(j):
        k = (p + j) % tp
        return [
            remote(pool.at[0, k, mine], buf.at[r, p, mine], s.at[0, k], s.at[1, p], {"tp": k})
            for pool, buf, s in ((shrink, a_buf, a_sems), (expand, e_buf, e_sems))
        ]

    def own_copies():
        return [
            pltpu.make_async_copy(pool.at[0, p, mine], buf.at[r, p, mine], s.at[1, p])
            for pool, buf, s in ((shrink, a_buf, a_sems), (expand, e_buf, e_sems))
        ]

    def across_copies(src, rows_of):
        return [
            remote(buf.at[r, src, rows_of], buf.at[r, src, rows_of],
                   s.at[2, src], s.at[3, src], across)
            for buf, s in ((a_buf, a_sems), (e_buf, e_sems))
        ]

    def sibling_copies(rep, src):
        return [
            remote(buf.at[rep, src], buf.at[rep, src], s.at[4, src], s.at[5, src], sibling)
            for buf, s in ((a_buf, a_sems), (e_buf, e_sems))
        ]

    def start_pages(j):
        for copy in page_copies(j + 1):
            copy.start()

    for copy in own_copies():
        copy.start()
    loop(tp - 1, start_pages)

    def product(n, store):
        @pl.when(n + 1 < total)
        def _():
            w_copy(n + 1).start()

        w_copy(n).wait()

        def piece(t):
            columns = pl.ds(pl.multiple_of(t * sub, sub), sub)
            store(columns, jnp.dot(
                hidden[...], w_buf[n % 2, :, columns], preferred_element_type=F32))

        loop(tile // sub, piece)

    def y_copy(u, j):
        device = {"tp": z * lo + (y + j) % lo}
        return remote(y_send.at[u, j - 1], y_recv.at[u, j - 1],
                      y_ssem.at[u, j - 1], y_rsem.at[u, j - 1], device)

    def send_tile(n):
        zz, c = unit(n // (lo - 1))
        j = 1 + n % (lo - 1)
        u = zz * per + c

        def store(columns, value):
            y_send[u, j - 1, :, columns] = value.astype(BF16)

        product(n, store)
        y_copy(u, j).start()

    loop(sends, send_tile)

    def forward(j):
        src = (p + tp - j) % tp

        @pl.when(j == 0)
        def _():
            for copy in own_copies():
                copy.wait()

        @pl.when(j > 0)
        def _():
            for pool, buf, s in ((shrink, a_buf, a_sems), (expand, e_buf, e_sems)):
                remote(pool.at[0, src, mine], buf.at[r, src, mine],
                       s.at[0, src], s.at[1, src], {"tp": src}).wait_recv()

        for copy in across_copies(src, mine):
            copy.start()

    def forward_some(t):
        steps = firsts + units
        lax.fori_loop(
            t * tp // steps, (t + 1) * tp // steps, lambda j, c: (forward(j), c)[1], 0)

    def step(u, zz, buf_s, buf_r, ssem, rsem, slot, value):
        start = jnp.where(zz > z, z == 0, z == hi - 1)

        @pl.when(start)
        def _():
            buf_s[u] = value().astype(BF16)

        @pl.when(jnp.logical_not(start))
        def _():
            arrived(buf_s, buf_r, ssem, rsem, u)
            buf_s[u] = (value() + buf_r[u].astype(F32)).astype(BF16)

        step_copy(u, zz, buf_s, buf_r, ssem, rsem, slot).start()

    def step_copy(u, zz, buf_s, buf_r, ssem, rsem, slot):
        nz = jnp.where(zz > z, z + 1, z - 1)
        target = jnp.where(jnp.logical_and(nz == zz, zz < z), slot, u)
        return remote(buf_s.at[u], buf_r.at[target], ssem.at[u], rsem.at[target],
                      {"tp": nz * lo + y})

    def arrived(buf_s, buf_r, ssem, rsem, slot):
        remote(buf_s.at[0], buf_r.at[slot], ssem.at[0], rsem.at[slot], across).wait_recv()

    def ends(buf_s, buf_r, ssem, rsem, u, slot, add):
        @pl.when(z > 0)
        def _():
            arrived(buf_s, buf_r, ssem, rsem, u)
            add(buf_r[u].astype(F32))

        @pl.when(z < hi - 1)
        def _():
            arrived(buf_s, buf_r, ssem, rsem, slot)
            add(buf_r[slot].astype(F32))

    firsts_of = (f_send, f_recv, f_ssem, f_rsem)

    def first_tile(m):
        zz, yy, c = first_unit(m)
        v = (zz * lo + yy) * zf + c

        def store(columns, value):
            f_own[v, :, columns] = value

        product(sends + m, store)
        forward_some(m)

    def first_step(m):
        zz, yy, c = first_unit(m)
        v = (zz * lo + yy) * zf + c

        @pl.when(zz != z)
        def _():
            step(v, zz, *firsts_of, firsts + yy * zf + c, lambda: f_own[v])

    def first_ends(yy, c):
        v = (z * lo + yy) * zf + c

        def add(value):
            f_own[v] += value

        ends(*firsts_of, v, firsts + yy * zf + c, add)
        return v

    def fy_copy(c, j):
        return remote(fy_send.at[c, j - 1], fy_recv.at[c, j - 1],
                      fy_sems.at[0, c, j - 1], fy_sems.at[1, c, j - 1],
                      {"tp": z * lo + (y + j) % lo})

    def first_across(i):
        c, j = i // (lo - 1), 1 + i % (lo - 1)
        v = first_ends((y + j) % lo, c)
        fy_send[c, j - 1] = f_own[v].astype(BF16)
        fy_copy(c, j).start()

    def first_finish(c):
        columns = pl.ds(pl.multiple_of((per + c) * tile, tile), tile)
        v = first_ends(y, c)
        out[:, columns] += f_own[v]
        for j in range(1, lo):
            fy_copy(c, j).wait_recv()
            out[:, columns] += fy_recv[c, j - 1].astype(F32)

    def keep_tile(i):
        zz, c = unit(i)
        u = zz * per + c

        def store(columns, value):
            keep[u, :, columns] = value

        product(sends + firsts + i, store)
        forward_some(firsts + i)

    if zf:
        loop(firsts, first_tile)
    loop(units, keep_tile)
    if zf:
        loop(firsts, first_step)

    def base(u):
        value = keep[u]
        for j in range(1, lo):
            value = value + y_recv[u, j - 1].astype(F32)
        return value

    def wait_y(u):
        for j in range(1, lo):
            y_copy(u, j).wait_recv()

    units_of = (z_send, z_recv, z_ssem, z_rsem)

    def pass_on(i):
        zz, c = unit(i)
        u = zz * per + c

        @pl.when(zz != z)
        def _():
            wait_y(u)
            step(u, zz, *units_of, units + c, lambda: base(u))

    def share_page(j):
        src = (p + tp - j) % tp
        for copy in across_copies(src, other):
            copy.wait_recv()
        for copy in sibling_copies(r, src):
            copy.start()

    early = units // 2
    loop(early, pass_on)
    if zf:
        loop(zf * (lo - 1), first_across)
    loop(tp, share_page)

    def wait_page(j):
        src = (p + tp - j) % tp
        for copy in sibling_copies(1 - r, src):
            copy.wait_recv()

    loop(tp, wait_page)
    quads = tp // 4
    lane = lax.broadcasted_iota(jnp.int32, (rows, 4 * rank), 1) // rank

    def chosen(i):
        return source[...] == lane + i * 4

    def shrink_quad(i):
        pages = a_buf[i // quads, pl.ds((i % quads) * 4, 4)].reshape(4 * rank, a_buf.shape[3])
        value = lax.dot_general(
            hidden[...], pages, (((1,), (1,)), ((), ())), preferred_element_type=F32)
        part[...] += jnp.where(chosen(i), value, 0.0)

    part[...] = jnp.zeros_like(part)
    middle = (units - early) * 2 // 3

    def quads_and_unit(t):
        lax.fori_loop(
            t * 2 * quads // middle, (t + 1) * 2 * quads // middle,
            lambda i, c: (shrink_quad(i), c)[1], 0)
        pass_on(early + t)

    loop(middle, quads_and_unit)
    folded = part[:, :2 * rank] + part[:, 2 * rank:]
    folded = folded + jnp.concatenate([folded[:, rank:], folded[:, :rank]], axis=1)
    part[:, :2 * rank] = folded

    def rows_of(k):
        return pl.ds(pl.multiple_of(k * share, share), share)

    def part_copy(j):
        k = (p + j) % tp
        return remote(part.at[rows_of(k), pl.ds(0, 2 * rank)], part_in.at[p],
                      c_sems.at[0, k], c_sems.at[1, p], {"tp": k})

    def part_arrived(src):
        return remote(part.at[rows_of(src), pl.ds(0, 2 * rank)], part_in.at[src],
                      c_sems.at[0, src], c_sems.at[1, src], {"tp": src})

    def code_copy(k, at):
        return remote(code_own, code.at[rows_of(at)],
                      c_sems.at[2, k], c_sems.at[3, at], {"tp": k})

    loop(tp - 1, lambda j: part_copy(j + 1).start())
    loop(units - early - middle, lambda i: pass_on(early + middle + i))

    code_own[...] = part[rows_of(p), :2 * rank]

    def add_part(j):
        src = (p + j + 1) % tp
        part_arrived(src).wait_recv()
        code_own[...] += part_in[src]

    loop(tp - 1, add_part)
    code_own[...] = code_own[...].astype(BF16).astype(F32)
    code[rows_of(p), :] = code_own[...]
    loop(tp - 1, lambda j: code_copy((p + j + 1) % tp, p).start())
    loop(tp - 1, lambda j: code_copy((p + j + 1) % tp, (p + j + 1) % tp).wait_recv())

    out[...] = jnp.zeros_like(out)

    def expand_quad(i):
        both = code[...]
        codes = jnp.where(chosen(i), jnp.concatenate([both, both], axis=1), 0.0).astype(BF16)
        pages = e_buf[i // quads, pl.ds((i % quads) * 4, 4)].reshape(4 * rank, width)
        out[...] += jnp.dot(codes, pages, preferred_element_type=F32)

    loop(2 * quads, expand_quad)

    def finish(c):
        u = z * per + c
        columns = pl.ds(pl.multiple_of(c * tile, tile), tile)
        wait_y(u)
        out[:, columns] += base(u)

        def add(value):
            out[:, columns] += value

        ends(*units_of, u, units + c, add)

    if zf:
        loop(zf, first_finish)
    loop(per, finish)

    def sent(i):
        zz, c = unit(i)
        u = zz * per + c
        for j in range(1, lo):
            y_copy(u, j).wait_send()

        @pl.when(zz != z)
        def _():
            step_copy(u, zz, *units_of, units + c).wait_send()

    loop(units, sent)

    def first_sent(m):
        zz, yy, c = first_unit(m)
        v = (zz * lo + yy) * zf + c

        @pl.when(zz != z)
        def _():
            step_copy(v, zz, *firsts_of, firsts + yy * zf + c).wait_send()

    if zf:
        loop(firsts, first_sent)
        loop(zf * (lo - 1), lambda i: fy_copy(i // (lo - 1), 1 + i % (lo - 1)).wait_send())

    def sent_pages(j):
        for copy in across_copies(j, mine) + sibling_copies(r, j):
            copy.wait_send()

        @pl.when(j > 0)
        def _():
            for copy in page_copies(j):
                copy.wait_send()
            part_copy(j).wait_send()
            code_copy((p + j) % tp, p).wait_send()

    loop(tp, sent_pages)


def per_device(
    hidden, down_weight, residual, pool_shrink, pool_expand, tenant_home, request_owner_tenant
):
    tp = lax.axis_size("tp")
    reps = lax.axis_size("rep")
    place = lax.axis_index("tp")
    requests, steps, units = hidden.shape
    width = residual.shape[2]
    rank = pool_shrink.shape[2]
    rows = requests * steps
    home_device = tenant_home // tp * tp + (tenant_home % tp + place) % tp
    tenants = tenant_home.shape[0]
    source = jnp.sum(
        jnp.where(request_owner_tenant == jnp.arange(tenants)[None, :], home_device[None, :], 0),
        axis=1, dtype=jnp.int32,
    )
    source = jnp.broadcast_to(source[:, None], (requests, steps)).reshape(rows, 1)
    lo = 1 << (int(math.log2(tp)) // 2)
    hi = tp // lo
    tile = max(128, width // 4)
    sub = min(256, tile)
    zf = width // tile // 4
    per = width // tile - zf
    n = hi * per
    few = max(zf, 1)
    m = tp * few
    dma = pltpu.SemaphoreType.DMA
    vmem = pl.BlockSpec(memory_space=pltpu.VMEM)
    hbm = pl.BlockSpec(memory_space=pl.ANY)
    added = pl.pallas_call(
        functools.partial(fused, tp, lo, hi, tile, sub, zf),
        out_shape=jax.ShapeDtypeStruct((rows, width), F32),
        in_specs=[vmem, hbm, hbm, hbm, vmem],
        out_specs=vmem,
        scratch_shapes=[
            pltpu.VMEM((2, units, tile), BF16),
            pltpu.VMEM((n, lo - 1, rows, tile), BF16),
            pltpu.VMEM((n, lo - 1, rows, tile), BF16),
            pltpu.VMEM((n, rows, tile), F32),
            pltpu.VMEM((n, rows, tile), BF16),
            pltpu.VMEM((n + per, rows, tile), BF16),
            pltpu.VMEM((m, rows, tile), F32),
            pltpu.VMEM((m, rows, tile), BF16),
            pltpu.VMEM((m + lo * few, rows, tile), BF16),
            pltpu.VMEM((few, lo - 1, rows, tile), BF16),
            pltpu.VMEM((few, lo - 1, rows, tile), BF16),
            pltpu.VMEM((reps, tp, rank, units), BF16),
            pltpu.VMEM((reps, tp, rank, width), BF16),
            pltpu.VMEM((rows, 4 * rank), F32),
            pltpu.VMEM((tp, rows // tp, 2 * rank), F32),
            pltpu.VMEM((rows, 2 * rank), F32),
            pltpu.VMEM((rows // tp, 2 * rank), F32),
            dma((2,)),
            dma((n, lo - 1)),
            dma((n, lo - 1)),
            dma((n,)),
            dma((n + per,)),
            dma((m,)),
            dma((m + lo * few,)),
            dma((2, few, lo - 1)),
            dma((6, tp)),
            dma((6, tp)),
            dma((4, tp)),
        ],
        compiler_params=pltpu.CompilerParams(
            collective_id=0, has_side_effects=True, vmem_limit_bytes=62 * 1024 * 1024
        ),
    )(hidden.reshape(rows, units), down_weight, pool_shrink, pool_expand, source)
    added = added.reshape(requests, steps, width)
    return (residual.astype(F32) + added).astype(BF16)


def solution(mesh):
    in_specs = (
        P(("groups", "rep"), None, "tp"),
        P("tp", None),
        P(("groups", "rep"), None, "tp"),
        P(("rep", "tp"), None, None, None),
        P(("rep", "tp"), None, None, None),
        P(),
        P(("groups", "rep"), None),
    )
    out_specs = P(("groups", "rep"), None, "tp")
    return jax.shard_map(
        per_device, mesh=mesh, in_specs=in_specs, out_specs=out_specs, check_vma=False
    )
```

```python
import functools
import math

import jax
import jax.numpy as jnp
from jax import lax
from jax.experimental import pallas as pl
from jax.experimental.pallas import tpu as pltpu
from jax.sharding import PartitionSpec as P

MESH = pl.DeviceIdType.MESH
F32 = jnp.float32
BF16 = jnp.bfloat16


def fused(
    tp, lo, hi, tile, sub,
    hidden, weight, shrink, expand, source, out,
    w_buf, y_send, y_recv, keep, z_send, z_recv, a_buf, e_buf, part, part_in, code, code_own,
    w_sem, y_ssem, y_rsem, z_ssem, z_rsem, a_sems, e_sems, c_sems,
):
    g, r, p = lax.axis_index("groups"), lax.axis_index("rep"), lax.axis_index("tp")
    z, y = p // lo, p % lo
    rows = hidden.shape[0]
    width = out.shape[1]
    per = width // tile
    units = hi * per
    rank = shrink.shape[2]
    half = rank // 2
    share = rows // tp
    across, sibling = {"groups": 1 - g}, {"rep": 1 - r}

    def remote(src, dst, ssem, rsem, device):
        return pltpu.make_async_remote_copy(
            src_ref=src, dst_ref=dst, send_sem=ssem, recv_sem=rsem,
            device_id=device, device_id_type=MESH,
        )

    def loop(n, body):
        lax.fori_loop(0, n, lambda i, c: (body(i), c)[1], 0)

    def peer(j):
        return {"tp": (p + j) % tp}

    barrier = pltpu.get_barrier_semaphore()
    loop(tp - 1, lambda j: pl.semaphore_signal(
        barrier, inc=1, device_id=peer(j + 1), device_id_type=MESH))
    pl.semaphore_signal(barrier, inc=1, device_id=across, device_id_type=MESH)
    pl.semaphore_signal(barrier, inc=1, device_id=sibling, device_id_type=MESH)

    def unit(i):
        q, c = i // per, i % per
        zz = jnp.where(q % 2 == 0, hi - 1 - q // 2, q // 2)
        return zz, c

    sends = units * (lo - 1)
    total = units * lo

    def tile_of(n):
        sending = n < sends
        i = jnp.where(sending, n // max(lo - 1, 1), n - sends)
        j = jnp.where(sending, 1 + n % max(lo - 1, 1), 0)
        zz, c = unit(i)
        return zz, c, j

    def w_copy(n):
        zz, c, j = tile_of(n)
        column = (zz * lo + (y + j) % lo) * width + c * tile
        return pltpu.make_async_copy(
            weight.at[:, pl.ds(pl.multiple_of(column, tile), tile)],
            w_buf.at[n % 2], w_sem.at[n % 2],
        )

    w_copy(0).start()
    pl.semaphore_wait(barrier, tp + 1)

    mine = pl.ds(pl.multiple_of(g * half, half), half)
    other = pl.ds(pl.multiple_of((1 - g) * half, half), half)

    def page_copies(j):
        k = (p + j) % tp
        return [
            remote(pool.at[0, k, mine], buf.at[r, p, mine], s.at[0, k], s.at[1, p], {"tp": k})
            for pool, buf, s in ((shrink, a_buf, a_sems), (expand, e_buf, e_sems))
        ]

    def own_copies():
        return [
            pltpu.make_async_copy(pool.at[0, p, mine], buf.at[r, p, mine], s.at[1, p])
            for pool, buf, s in ((shrink, a_buf, a_sems), (expand, e_buf, e_sems))
        ]

    def across_copies(src, rows_of):
        return [
            remote(buf.at[r, src, rows_of], buf.at[r, src, rows_of],
                   s.at[2, src], s.at[3, src], across)
            for buf, s in ((a_buf, a_sems), (e_buf, e_sems))
        ]

    def sibling_copies(rep, src):
        return [
            remote(buf.at[rep, src], buf.at[rep, src], s.at[4, src], s.at[5, src], sibling)
            for buf, s in ((a_buf, a_sems), (e_buf, e_sems))
        ]

    def start_pages(j):
        for copy in page_copies(j + 1):
            copy.start()

    for copy in own_copies():
        copy.start()
    loop(tp - 1, start_pages)

    def product(n, store):
        @pl.when(n + 1 < total)
        def _():
            w_copy(n + 1).start()

        w_copy(n).wait()

        def piece(t):
            columns = pl.ds(pl.multiple_of(t * sub, sub), sub)
            store(columns, jnp.dot(
                hidden[...], w_buf[n % 2, :, columns], preferred_element_type=F32))

        loop(tile // sub, piece)

    def y_copy(u, j):
        device = {"tp": z * lo + (y + j) % lo}
        return remote(y_send.at[u, j - 1], y_recv.at[u, j - 1],
                      y_ssem.at[u, j - 1], y_rsem.at[u, j - 1], device)

    def send_tile(n):
        zz, c, j = tile_of(n)
        u = zz * per + c

        def store(columns, value):
            y_send[u, j - 1, :, columns] = value.astype(BF16)

        product(n, store)
        y_copy(u, j).start()

    loop(sends, send_tile)

    def forward(j):
        src = (p + tp - j) % tp

        @pl.when(j == 0)
        def _():
            for copy in own_copies():
                copy.wait()

        @pl.when(j > 0)
        def _():
            for pool, buf, s in ((shrink, a_buf, a_sems), (expand, e_buf, e_sems)):
                remote(pool.at[0, src, mine], buf.at[r, src, mine],
                       s.at[0, src], s.at[1, src], {"tp": src}).wait_recv()

        for copy in across_copies(src, mine):
            copy.start()

    def keep_tile(i):
        zz, c = unit(i)
        u = zz * per + c

        def store(columns, value):
            keep[u, :, columns] = value

        product(sends + i, store)
        loop(tp // units, lambda t: forward(i * (tp // units) + t))

    loop(units, keep_tile)

    def base(u):
        value = keep[u]
        for j in range(1, lo):
            value = value + y_recv[u, j - 1].astype(F32)
        return value

    def wait_y(u):
        for j in range(1, lo):
            y_copy(u, j).wait_recv()

    def z_copy(u, zz, c):
        nz = jnp.where(zz > z, z + 1, z - 1)
        slot = jnp.where((nz == zz) & (zz < z), units + c, u)
        return remote(z_send.at[u], z_recv.at[slot], z_ssem.at[u], z_rsem.at[slot],
                      {"tp": nz * lo + y})

    def z_arrived(slot):
        remote(z_send.at[0], z_recv.at[slot], z_ssem.at[0], z_rsem.at[slot],
               across).wait_recv()

    def pass_on(i):
        zz, c = unit(i)
        u = zz * per + c
        first = jnp.where(zz > z, z == 0, z == hi - 1)

        @pl.when(zz != z)
        def _():
            wait_y(u)

            @pl.when(first)
            def _():
                z_send[u] = base(u).astype(BF16)

            @pl.when(jnp.logical_not(first))
            def _():
                z_arrived(u)
                z_send[u] = (base(u) + z_recv[u].astype(F32)).astype(BF16)

            z_copy(u, zz, c).start()

    def share_page(j):
        src = (p + tp - j) % tp
        for copy in across_copies(src, other):
            copy.wait_recv()
        for copy in sibling_copies(r, src):
            copy.start()

    early = units // 2
    loop(early, pass_on)
    loop(tp, share_page)
    later = units // 4
    loop(later, lambda i: pass_on(early + i))

    def wait_page(j):
        src = (p + tp - j) % tp
        for copy in sibling_copies(1 - r, src):
            copy.wait_recv()

    loop(tp, wait_page)
    quads = tp // 4
    lane = lax.broadcasted_iota(jnp.int32, (rows, 4 * rank), 1) // rank

    def chosen(i):
        return source[...] == lane + i * 4

    def shrink_quad(i):
        pages = a_buf[i // quads, pl.ds((i % quads) * 4, 4)].reshape(4 * rank, a_buf.shape[3])
        value = lax.dot_general(
            hidden[...], pages, (((1,), (1,)), ((), ())), preferred_element_type=F32)
        part[...] += jnp.where(chosen(i), value, 0.0)

    part[...] = jnp.zeros_like(part)
    loop(2 * quads, shrink_quad)
    folded = part[:, :2 * rank] + part[:, 2 * rank:]
    folded = folded + jnp.concatenate([folded[:, rank:], folded[:, :rank]], axis=1)
    part[:, :2 * rank] = folded

    def rows_of(k):
        return pl.ds(pl.multiple_of(k * share, share), share)

    def part_copy(j):
        k = (p + j) % tp
        return remote(part.at[rows_of(k), pl.ds(0, 2 * rank)], part_in.at[p],
                      c_sems.at[0, k], c_sems.at[1, p], {"tp": k})

    def part_arrived(src):
        return remote(part.at[rows_of(src), pl.ds(0, 2 * rank)], part_in.at[src],
                      c_sems.at[0, src], c_sems.at[1, src], {"tp": src})

    def code_copy(k, at):
        return remote(code_own, code.at[rows_of(at)],
                      c_sems.at[2, k], c_sems.at[3, at], {"tp": k})

    loop(tp - 1, lambda j: part_copy(j + 1).start())
    loop(units - early - later, lambda i: pass_on(early + later + i))

    code_own[...] = part[rows_of(p), :2 * rank]

    def add_part(j):
        src = (p + j + 1) % tp
        part_arrived(src).wait_recv()
        code_own[...] += part_in[src]

    loop(tp - 1, add_part)
    code_own[...] = code_own[...].astype(BF16).astype(F32)
    code[rows_of(p), :] = code_own[...]
    loop(tp - 1, lambda j: code_copy((p + j + 1) % tp, p).start())
    loop(tp - 1, lambda j: code_copy((p + j + 1) % tp, (p + j + 1) % tp).wait_recv())

    out[...] = jnp.zeros_like(out)

    def expand_quad(i):
        both = code[...]
        codes = jnp.where(chosen(i), jnp.concatenate([both, both], axis=1), 0.0).astype(BF16)
        pages = e_buf[i // quads, pl.ds((i % quads) * 4, 4)].reshape(4 * rank, width)
        out[...] += jnp.dot(codes, pages, preferred_element_type=F32)

    loop(2 * quads, expand_quad)

    def finish(c):
        u = z * per + c
        columns = pl.ds(pl.multiple_of(c * tile, tile), tile)
        wait_y(u)
        out[:, columns] += base(u)

        @pl.when(z > 0)
        def _():
            z_arrived(u)
            out[:, columns] += z_recv[u].astype(F32)

        @pl.when(z < hi - 1)
        def _():
            z_arrived(units + c)
            out[:, columns] += z_recv[units + c].astype(F32)

    loop(per, finish)

    def sent(i):
        zz, c = unit(i)
        u = zz * per + c
        for j in range(1, lo):
            y_copy(u, j).wait_send()

        @pl.when(zz != z)
        def _():
            z_copy(u, zz, c).wait_send()

    loop(units, sent)

    def sent_pages(j):
        for copy in across_copies(j, mine) + sibling_copies(r, j):
            copy.wait_send()

        @pl.when(j > 0)
        def _():
            for copy in page_copies(j):
                copy.wait_send()
            part_copy(j).wait_send()
            code_copy((p + j) % tp, p).wait_send()

    loop(tp, sent_pages)


def per_device(
    hidden, down_weight, residual, pool_shrink, pool_expand, tenant_home, request_owner_tenant
):
    tp = lax.axis_size("tp")
    reps = lax.axis_size("rep")
    place = lax.axis_index("tp")
    requests, steps, units = hidden.shape
    width = residual.shape[2]
    rank = pool_shrink.shape[2]
    rows = requests * steps
    home_device = tenant_home // tp * tp + (tenant_home % tp + place) % tp
    tenants = tenant_home.shape[0]
    source = jnp.sum(
        jnp.where(request_owner_tenant == jnp.arange(tenants)[None, :], home_device[None, :], 0),
        axis=1, dtype=jnp.int32,
    )
    source = jnp.broadcast_to(source[:, None], (requests, steps)).reshape(rows, 1)
    lo = 1 << (int(math.log2(tp)) // 2)
    hi = tp // lo
    tile = min(512, width)
    sub = min(256, tile)
    per = width // tile
    n = hi * per
    dma = pltpu.SemaphoreType.DMA
    vmem = pl.BlockSpec(memory_space=pltpu.VMEM)
    hbm = pl.BlockSpec(memory_space=pl.ANY)
    added = pl.pallas_call(
        functools.partial(fused, tp, lo, hi, tile, sub),
        out_shape=jax.ShapeDtypeStruct((rows, width), F32),
        in_specs=[vmem, hbm, hbm, hbm, vmem],
        out_specs=vmem,
        scratch_shapes=[
            pltpu.VMEM((2, units, tile), BF16),
            pltpu.VMEM((n, lo - 1, rows, tile), BF16),
            pltpu.VMEM((n, lo - 1, rows, tile), BF16),
            pltpu.VMEM((n, rows, tile), F32),
            pltpu.VMEM((n, rows, tile), BF16),
            pltpu.VMEM((n + per, rows, tile), BF16),
            pltpu.VMEM((reps, tp, rank, units), BF16),
            pltpu.VMEM((reps, tp, rank, width), BF16),
            pltpu.VMEM((rows, 4 * rank), F32),
            pltpu.VMEM((tp, rows // tp, 2 * rank), F32),
            pltpu.VMEM((rows, 2 * rank), F32),
            pltpu.VMEM((rows // tp, 2 * rank), F32),
            dma((2,)),
            dma((n, lo - 1)),
            dma((n, lo - 1)),
            dma((n,)),
            dma((n + per,)),
            dma((6, tp)),
            dma((6, tp)),
            dma((4, tp)),
        ],
        compiler_params=pltpu.CompilerParams(
            collective_id=0, has_side_effects=True, vmem_limit_bytes=62 * 1024 * 1024
        ),
    )(hidden.reshape(rows, units), down_weight, pool_shrink, pool_expand, source)
    added = added.reshape(requests, steps, width)
    return (residual.astype(F32) + added).astype(BF16)


def solution(mesh):
    in_specs = (
        P(("groups", "rep"), None, "tp"),
        P("tp", None),
        P(("groups", "rep"), None, "tp"),
        P(("rep", "tp"), None, None, None),
        P(("rep", "tp"), None, None, None),
        P(),
        P(("groups", "rep"), None),
    )
    out_specs = P(("groups", "rep"), None, "tp")
    return jax.shard_map(
        per_device, mesh=mesh, in_specs=in_specs, out_specs=out_specs, check_vma=False
    )
```
